256 devices in a mesh: lon: 16 (over x_hi, y, core), lat: 16 (over x_lo, z).
Axes of the slice: x: 4 (x_hi: 2, x_lo: 2; x = x_hi * 2 + x_lo), y: 4, z: 8, core: 2. Of those that a mesh axis runs over, the one named last changes fastest.
Arguments:
- zonal_current: float32 [4096, 32768], P('lon', 'lat'), may hold values from -6 to 6
- meridional_current: float32 [4096, 32768], P('lon', 'lat'), may hold values from -6 to 6
- thermal_departure: float32 [4096, 32768], P('lon', 'lat'), may hold values from -6 to 6
- wet_point_flag: int32 [4096, 32768], P('lon', 'lat'), may hold values 0 or 1
Outputs:
- flux_east: float32 [4096, 32768], P('lon', 'lat')
- flux_north: float32 [4096, 32768], P('lon', 'lat')
The draws below stay inside these ranges and needn't reach their ends.
All inputs are finite; a program needn't handle non-finite values. No bound on the sum of `wet_point_flag` on one device may be relied on, other than what follows from the above.
Results may differ from the reference program's by a relative error of at most 0.0003.
Values sent between devices are 32-bit elements; how exact they have to be, the bound alone decides.
No kernel may reach another device: no remote copies, remote signals or barrier semaphores. Data moves between devices by JAX's collectives and lax.ppermute only.
A program may use at most 192 MiB of HBM per device.

```python
import jax
import jax.numpy as jnp
from jax import lax

HALF = 64
MERIDIAN_TOTAL = 4096
PARALLEL_TOTAL = 32768


def draw_thermal_departure(key, part):
    noise = jax.random.normal(key, (MERIDIAN_TOTAL, PARALLEL_TOTAL), jnp.float32)
    return jnp.clip(3.0 + noise, -6.0, 6.0).astype(jnp.float32)


def set_ends(drawn, own_key, smallest, largest):
    longest = drawn.shape.index(max(drawn.shape))
    spots = []
    for shift in (0, 1):
        where = [jax.random.randint(jax.random.fold_in(own_key, axis), (), 0, length) for axis, length in enumerate(drawn.shape)]
        where[longest] = (where[longest] + shift) % drawn.shape[longest]
        spots.append(tuple(where))
    return drawn.at[spots[0]].set(smallest).at[spots[1]].set(largest)


def level_of(own_key, shape, pieces, low, largest):
    gain, own = 1.0, jax.random.fold_in(own_key, 6)
    for position, blocks in pieces:
        heights = jnp.exp(jax.random.uniform(jax.random.fold_in(own, position), (blocks,), jnp.float32, low / len(pieces), largest / len(pieces)))
        gain = gain * jnp.repeat(heights, shape[position] // blocks).reshape([-1 if axis == position else 1 for axis in range(len(shape))])
    return gain


def scatter_about(key, extent, deviation, limit, cuts=(), kind=jnp.bfloat16):
    entries = jax.random.normal(key, extent, jnp.float32) * deviation
    if len(cuts) > 0:
        entries = level_of(key, extent, cuts, -0.22, 0.18) * entries
    return jnp.clip(entries, min=-limit, max=limit).astype(kind)


def setup_inputs(seed: int = 0) -> dict:
    key_of = jax.random.split(jax.random.key(seed), 5)
    zonal_current = scatter_about(key_of[0], (MERIDIAN_TOTAL, PARALLEL_TOTAL), 1.0, 6.0, ((0, 16), (1, 16)), jnp.float32)
    meridional_current = scatter_about(key_of[1], (MERIDIAN_TOTAL, PARALLEL_TOTAL), 1.0, 6.0, ((0, 16), (1, 16)), jnp.float32)
    thermal_departure = draw_thermal_departure(jax.random.fold_in(key_of[4], 71), 0)
    wet_point_flag = set_ends((jax.random.randint(key_of[3], (MERIDIAN_TOTAL, PARALLEL_TOTAL), 0, 4) < 3).astype(jnp.int32), jax.random.fold_in(key_of[3], 1), 0, 1)
    return dict(zonal_current=zonal_current, meridional_current=meridional_current, thermal_departure=thermal_departure, wet_point_flag=wet_point_flag)


def band_matrix():
    block_len = 2 * HALF
    sigma = HALF / 2.0
    offsets = jnp.arange(2 * HALF + 1, dtype=jnp.float32) - HALF
    weight_sum = jnp.sum(jnp.exp(-offsets * offsets / (2.0 * sigma * sigma)))
    rows = jnp.arange(block_len, dtype=jnp.int32)[:, None]
    cols = jnp.arange(2 * block_len, dtype=jnp.int32)[None, :]
    dist = (cols - rows).astype(jnp.float32) - HALF
    inside = (cols - rows >= 0) & (cols - rows <= 2 * HALF)
    weights_band = jnp.where(inside, jnp.exp(-dist * dist / (2.0 * sigma * sigma)) / weight_sum, 0.0)
    taps_norm = jnp.exp(-offsets * offsets / (2.0 * sigma * sigma)) / weight_sum
    flux_scale = 1.0 / (jnp.sum(taps_norm * taps_norm) ** 2)
    return weights_band.astype(jnp.float32), flux_scale.astype(jnp.float32)


def filter_last(padded, weights_band):
    block_len = 2 * HALF
    length = padded.shape[-1] - block_len
    lead = padded.shape[:-1]
    leading = padded[..., :length].reshape(lead + (length // block_len, block_len))
    trailing = padded[..., block_len:].reshape(lead + (length // block_len, block_len))
    windows = jnp.concatenate([leading, trailing], axis=-1)
    result = jnp.einsum('...bj,ij->...bi', windows, weights_band, precision=lax.Precision.HIGHEST)
    return result.reshape(lead + (length,))


def heat_fluxes(filtered, flux_scale):
    east = flux_scale * (filtered[3] - filtered[0] * filtered[2])
    north = flux_scale * (filtered[4] - filtered[1] * filtered[2])
    return jnp.stack([east, north])


def reference(zonal_current, meridional_current, thermal_departure, wet_point_flag):
    wet_cell_weights = wet_point_flag.astype(jnp.float32)
    layered_quantities = jnp.stack([wet_cell_weights * zonal_current, wet_cell_weights * meridional_current, wet_cell_weights * thermal_departure])
    padded = jnp.concatenate([layered_quantities[:, -HALF:], layered_quantities, layered_quantities[:, :HALF]], axis=1)
    weights_band, flux_scale = band_matrix()
    block_len = 2 * HALF
    nblocks = MERIDIAN_TOTAL // block_len

    def one_block(index):
        windows = lax.dynamic_slice_in_dim(padded, index * block_len, 2 * block_len, axis=1)
        fields = jnp.concatenate([windows, windows[0:1] * windows[2:3], windows[1:2] * windows[2:3]], axis=0)
        zonal_done = jnp.einsum('ij,fjr->fir', weights_band, fields, precision=lax.Precision.HIGHEST)
        rimmed = jnp.pad(zonal_done, ((0, 0), (0, 0), (HALF, HALF)))
        filtered = filter_last(rimmed, weights_band)
        return heat_fluxes(filtered, flux_scale)

    blocks = lax.map(one_block, jnp.arange(nblocks, dtype=jnp.int32))
    result = jnp.transpose(blocks, (1, 0, 2, 3)).reshape(2, MERIDIAN_TOTAL, PARALLEL_TOTAL)
    return result[0], result[1]
```

```python
import functools

import jax
import jax.numpy as jnp
import ml_dtypes
import numpy as np
from jax import lax
from jax.experimental import pallas as pl
from jax.experimental.pallas import tpu as pltpu
from jax.sharding import PartitionSpec as P

HALF = 64
BLK = 2 * HALF
ROWS = 256
COLS = 2048
NB = COLS // BLK
EXT = COLS + BLK
CW = 256
NJ = COLS // CW
MID = ROWS - BLK
SPLIT = 1280
BF = jnp.bfloat16
F32 = jnp.float32


def taps_np():
    k = np.arange(-HALF, HALF + 1, dtype=np.float64)
    sigma = HALF / 2.0
    g = np.exp(-k * k / (2.0 * sigma * sigma))
    return g / g.sum()


def toeplitz(rows, cols, shift):
    g = taps_np()
    k = np.arange(cols)[None, :] - np.arange(rows)[:, None] + shift
    return np.where(np.abs(k) <= HALF, g[np.clip(k + HALF, 0, 2 * HALF)], 0.0)


def hi_lo(a):
    a = a.astype(np.float32)
    hi = a.astype(ml_dtypes.bfloat16)
    lo = (a - hi.astype(np.float32)).astype(ml_dtypes.bfloat16)
    return hi, lo


SCALE = float(1.0 / np.sum(taps_np() ** 2) ** 2)


def split(x):
    hi = x.astype(BF)
    lo = (x - hi.astype(F32)).astype(BF)
    return hi, lo


def dot(a, b):
    return jnp.dot(a, b, preferred_element_type=F32)


def five(u, v, t):
    return (u, v, t, u * t, v * t)


def lat_window(zh, zl, w, start, rows):
    cols = pl.ds(start, 2 * BLK)
    r = dot(zh[:, cols], w) + dot(zl[:, cols], w)
    f = (r[:, :BLK] + r[:, BLK:]).reshape(5, rows, BLK)
    east = SCALE * (f[3] - f[0] * f[2])
    north = SCALE * (f[4] - f[1] * f[2])
    return pltpu.roll(east, HALF, 1), pltpu.roll(north, HALF, 1)


def first_half(shape):
    return lax.broadcasted_iota(jnp.int32, shape, 1) < HALF


def lat_pair(zh, zl, w, carry, fo, j, rows):
    low = first_half((rows, BLK))
    base = pl.multiple_of(j * CW, CW)
    pair0 = lat_window(zh, zl, w, base, rows)
    pair1 = lat_window(zh, zl, w, base + BLK, rows)
    for q in range(2):
        fo[q, :, pl.ds(base, BLK)] = jnp.where(low, carry[q], pair0[q])
        fo[q, :, pl.ds(base + BLK, BLK)] = jnp.where(low, pair0[q], pair1[q])
        carry[q] = pair1[q]


def lat_last(zh, zl, w, carry, fo, rows):
    low = first_half((rows, BLK))
    pair = lat_window(zh, zl, w, COLS, rows)
    for q in range(2):
        fo[q, :, pl.ds(COLS, BLK)] = jnp.where(low, carry[q], pair[q])


def interior_kernel(u, v, t, m, wrap, g, w_ref, e_out, n_out, zp_out,
                    ub, vb, tb, mb, zh, zl, zps, fo, carry, sem_in, sem_out, sem_e, sem_n):
    w = w_ref[...]

    def in_copies(j):
        cols = pl.ds(pl.multiple_of(j * CW, CW), CW)
        return [
            pltpu.make_async_copy(src.at[:, cols], dst.at[:, cols], sem_in.at[i, j])
            for i, (src, dst) in enumerate(((u, ub), (v, vb), (t, tb), (m, mb)))
        ]

    def zp_copy(j):
        cols = pl.ds(pl.multiple_of(j * CW, CW), CW)
        return pltpu.make_async_copy(zps.at[:, :, cols], zp_out.at[:, :, cols], sem_out.at[j])

    def out_copies(j):
        src = pl.ds(pl.multiple_of(j * CW, BLK), CW)
        dst = pl.ds(pl.multiple_of(j * CW - BLK, BLK), CW)
        rows = pl.ds(HALF, MID)
        return [
            pltpu.make_async_copy(fo.at[0, :, src], e_out.at[rows, dst], sem_e.at[j]),
            pltpu.make_async_copy(fo.at[1, :, src], n_out.at[rows, dst], sem_n.at[j]),
        ]

    def end_copies():
        rows = pl.ds(HALF, MID)
        done = []
        for q, (out, sem) in enumerate(((e_out, sem_e), (n_out, sem_n))):
            done.append(pltpu.make_async_copy(
                fo.at[q, :, pl.ds(BLK, BLK)], out.at[rows, pl.ds(0, BLK)], sem.at[0]))
            done.append(pltpu.make_async_copy(
                fo.at[q, :, pl.ds(COLS, BLK)], out.at[rows, pl.ds(COLS - BLK, BLK)], sem.at[NJ]))
        return done

    def zonal_fields(fields, stores, zcols, width):
        ghl = g[...]
        for f, x in enumerate(fields):
            hi, lo = split(x)
            r = dot(ghl, hi)
            z = r[:ROWS] + r[ROWS:] + dot(ghl[:ROWS], lo)
            zps[f, 0:HALF, zcols] = z[0:HALF]
            zps[f, HALF:BLK, zcols] = z[ROWS - HALF:]
            a, b = split(z[HALF:ROWS - HALF])
            for s in stores:
                zh[f * MID:(f + 1) * MID, s] = a
                zl[f * MID:(f + 1) * MID, s] = b

    def zonal(j):
        cols = pl.ds(pl.multiple_of(j * CW, CW), CW)
        wet = mb[:, cols].astype(F32)
        fields = five(wet * ub[:, cols], wet * vb[:, cols], wet * tb[:, cols])
        zonal_fields(fields, [pl.ds(pl.multiple_of(j * CW + BLK, BLK), CW)], cols, CW)

    for j in range(NJ):
        for copy in in_copies(j):
            copy.start()
    zonal_fields(five(wrap[0], wrap[1], wrap[2]), [pl.ds(0, BLK), pl.ds(COLS + BLK, BLK)], pl.ds(COLS, BLK), BLK)
    wrap_copy = pltpu.make_async_copy(
        zps.at[:, :, pl.ds(COLS, BLK)], zp_out.at[:, :, pl.ds(COLS, BLK)], sem_out.at[NJ])
    wrap_copy.start()

    def arrive(j):
        for copy in in_copies(j):
            copy.wait()

    arrive(0)
    zonal(0)
    zp_copy(0).start()

    def step(j, _):
        arrive(j)
        lat_pair(zh, zl, w, carry, fo, j - 1, MID)
        zonal(j)
        zp_copy(j).start()

        @pl.when(j > 1)
        def _():
            for copy in out_copies(j - 1):
                copy.start()

        return 0

    lax.fori_loop(1, NJ, step, 0)
    lat_pair(zh, zl, w, carry, fo, NJ - 1, MID)
    for copy in out_copies(NJ - 1):
        copy.start()
    lat_last(zh, zl, w, carry, fo, MID)
    for copy in end_copies():
        copy.start()
    wrap_copy.wait()
    for j in range(NJ):
        zp_copy(j).wait()
    for j in range(1, NJ):
        for copy in out_copies(j):
            copy.wait()
    for copy in end_copies():
        copy.wait()


def edge_kernel(npieces, *refs):
    sel_ref, e_in, n_in, zp = refs[:4]
    pieces = refs[4:4 + npieces]
    (gx, w_ref, e_out, n_out, hb, zpb, zh, zl, fo, carry,
     sem_h, sem_z, sem_e, sem_n) = refs[4 + npieces:]
    sel = sel_ref[0]
    w = w_ref[...]
    zrow = pl.multiple_of(sel * HALF, HALF)
    orow = pl.multiple_of(sel * (ROWS - HALF), HALF)
    starts = [0]
    for p in pieces:
        starts.append(starts[-1] + p.shape[2])
    chunks = [(COLS, BLK)] + [(j * CW, CW) for j in range(NJ)]

    def copies(i):
        start, width = chunks[i]
        for p, s in zip(pieces, starts):
            if s <= start and start + width <= s + p.shape[2]:
                return [
                    pltpu.make_async_copy(
                        p.at[:, :, pl.ds(start - s, width)], hb.at[:, :, pl.ds(start, width)], sem_h.at[i]),
                    pltpu.make_async_copy(
                        zp.at[:, pl.ds(zrow, HALF), pl.ds(start, width)],
                        zpb.at[:, :, pl.ds(start, width)], sem_z.at[i]),
                ]
        raise ValueError(start)

    for i in range(NJ + 1):
        for copy in copies(i):
            copy.start()
    gmat = gx[sel]

    def zonal_chunk(cols, stores):
        for f, x in enumerate(five(hb[0, :, cols], hb[1, :, cols], hb[2, :, cols])):
            hi, lo = split(x)
            z = zpb[f, :, cols] + dot(gmat, jnp.concatenate([hi, lo, hi], axis=0))
            a, b = split(z)
            for s in stores:
                zh[f * HALF:(f + 1) * HALF, s] = a
                zl[f * HALF:(f + 1) * HALF, s] = b

    def out_copies(j):
        src = pl.ds(j * CW, CW)
        dst = pl.ds(j * CW - BLK, CW)
        rows = pl.ds(orow, HALF)
        return [
            pltpu.make_async_copy(fo.at[0, :, src], e_out.at[rows, dst], sem_e.at[j]),
            pltpu.make_async_copy(fo.at[1, :, src], n_out.at[rows, dst], sem_n.at[j]),
        ]

    def end_copies():
        rows = pl.ds(orow, HALF)
        done = []
        for q, (out, sem) in enumerate(((e_out, sem_e), (n_out, sem_n))):
            done.append(pltpu.make_async_copy(
                fo.at[q, :, pl.ds(BLK, BLK)], out.at[rows, pl.ds(0, BLK)], sem.at[0]))
            done.append(pltpu.make_async_copy(
                fo.at[q, :, pl.ds(COLS, BLK)], out.at[rows, pl.ds(COLS - BLK, BLK)], sem.at[NJ]))
        return done

    for copy in copies(0):
        copy.wait()
    zonal_chunk(pl.ds(COLS, BLK), [pl.ds(0, BLK), pl.ds(COLS + BLK, BLK)])
    for j in range(NJ):
        for copy in copies(j + 1):
            copy.wait()
        zonal_chunk(pl.ds(j * CW, CW), [pl.ds(j * CW + BLK, CW)])
        lat_pair(zh, zl, w, carry, fo, j, HALF)
        if j > 0:
            for copy in out_copies(j):
                copy.start()
    lat_last(zh, zl, w, carry, fo, HALF)
    for copy in end_copies():
        copy.start()
    for j in range(1, NJ):
        for copy in out_copies(j):
            copy.wait()
    for copy in end_copies():
        copy.wait()


ANY = pl.BlockSpec(memory_space=pl.ANY)
VMEM = pl.BlockSpec(memory_space=pltpu.VMEM)
SMEM = pl.BlockSpec(memory_space=pltpu.SMEM)


def lat_matrix():
    hi, lo = hi_lo(toeplitz(BLK, 2 * BLK, -HALF).T)
    return jnp.asarray(np.concatenate([hi, lo], axis=1))


def interior(u, v, t, m, wrap):
    hi, lo = hi_lo(toeplitz(ROWS, ROWS, 0))
    g = jnp.asarray(np.concatenate([hi, lo], axis=0))
    flux = jax.ShapeDtypeStruct((ROWS, COLS), F32)
    return pl.pallas_call(
        interior_kernel,
        out_shape=(flux, flux, jax.ShapeDtypeStruct((5, BLK, EXT), F32)),
        in_specs=[ANY] * 4 + [VMEM] * 3,
        out_specs=(ANY, ANY, ANY),
        scratch_shapes=[
            pltpu.VMEM((ROWS, COLS), F32),
            pltpu.VMEM((ROWS, COLS), F32),
            pltpu.VMEM((ROWS, COLS), F32),
            pltpu.VMEM((ROWS, COLS), jnp.int32),
            pltpu.VMEM((5 * MID, EXT + BLK), BF),
            pltpu.VMEM((5 * MID, EXT + BLK), BF),
            pltpu.VMEM((5, BLK, EXT), F32),
            pltpu.VMEM((2, MID, EXT), F32),
            pltpu.VMEM((2, MID, BLK), F32),
            pltpu.SemaphoreType.DMA((4, NJ)),
            pltpu.SemaphoreType.DMA((NJ + 1,)),
            pltpu.SemaphoreType.DMA((NJ + 1,)),
            pltpu.SemaphoreType.DMA((NJ + 1,)),
        ],
        compiler_params=pltpu.CompilerParams(vmem_limit_bytes=40 * 2**20),
        cost_estimate=pl.CostEstimate(flops=7_000_000_000, bytes_accessed=16 * 2**20, transcendentals=0),
        name="interior",
    )(u, v, t, m, wrap, g, lat_matrix())


def edge(sel, east, north, zp, pieces, name):
    mats = []
    for shift in (-HALF, HALF):
        hi, lo = hi_lo(toeplitz(HALF, HALF, shift))
        mats.append(np.concatenate([hi, hi, lo], axis=1))
    gx = jnp.asarray(np.stack(mats))
    flux = jax.ShapeDtypeStruct((ROWS, COLS), F32)
    return pl.pallas_call(
        functools.partial(edge_kernel, len(pieces)),
        out_shape=(flux, flux),
        in_specs=[SMEM] + [ANY] * (3 + len(pieces)) + [VMEM] * 2,
        out_specs=(ANY, ANY),
        scratch_shapes=[
            pltpu.VMEM((3, HALF, EXT), F32),
            pltpu.VMEM((5, HALF, EXT), F32),
            pltpu.VMEM((5 * HALF, EXT + BLK), BF),
            pltpu.VMEM((5 * HALF, EXT + BLK), BF),
            pltpu.VMEM((2, HALF, EXT), F32),
            pltpu.VMEM((2, HALF, BLK), F32),
            pltpu.SemaphoreType.DMA((NJ + 1,)),
            pltpu.SemaphoreType.DMA((NJ + 1,)),
            pltpu.SemaphoreType.DMA((NJ + 1,)),
            pltpu.SemaphoreType.DMA((NJ + 1,)),
        ],
        input_output_aliases={1: 0, 2: 1},
        compiler_params=pltpu.CompilerParams(vmem_limit_bytes=40 * 2**20),
        cost_estimate=pl.CostEstimate(flops=2_000_000_000, bytes_accessed=5 * 2**20, transcendentals=0),
        name=name,
    )(sel, east, north, zp, *pieces, gx, lat_matrix())


def shards(u, v, t, m):
    nlon, nlat = lax.axis_size("lon"), lax.axis_size("lat")
    core = lax.axis_index("lon") % 2
    xoff = core * (ROWS - HALF)
    ioff = (1 - core) * (ROWS - HALF)
    across = [(i, (i + 1) % nlon if i % 2 else (i - 1) % nlon) for i in range(nlon)]
    inside = [(i, i + 1 - 2 * (i % 2)) for i in range(nlon)]
    up = [(i, i + 1) for i in range(nlat - 1)]
    down = [(j, i) for i, j in up]

    def masked(row, nrows, lo, hi):
        def cut(a):
            return lax.dynamic_slice(a, (row, lo), (nrows, hi - lo))

        wet = cut(m).astype(F32)
        return jnp.stack([wet * cut(u), wet * cut(v), wet * cut(t)])

    x1 = lax.ppermute(masked(xoff, HALF, 0, SPLIT), "lon", across)
    from_left = lax.ppermute(masked(0, ROWS, COLS - BLK, COLS), "lat", up)
    from_right = lax.ppermute(masked(0, ROWS, 0, BLK), "lat", down)
    lane = lax.broadcasted_iota(jnp.int32, (3, ROWS, BLK), 2)
    wrap = jnp.where(lane < HALF, from_right, from_left)

    def corner(row):
        return lax.dynamic_slice(wrap, (0, row, 0), (3, HALF, BLK))

    x2 = jnp.concatenate([masked(xoff, HALF, SPLIT, COLS), corner(xoff)], axis=2)
    x2 = lax.ppermute(x2, "lon", across)
    near = jnp.concatenate([masked(ioff, HALF, 0, COLS), corner(ioff)], axis=2)
    near = lax.ppermute(near, "lon", inside)
    east, north, zp = interior(u, v, t, m, wrap)
    sel = core.astype(jnp.int32).reshape(1)
    east, north = edge(1 - sel, east, north, zp, (near,), "edge_near")
    return edge(sel, east, north, zp, (x1, x2), "edge_far")


def solution(mesh):
    return jax.shard_map(
        shards,
        mesh=mesh,
        in_specs=(P("lon", "lat"),) * 4,
        out_specs=(P("lon", "lat"),) * 2,
        check_vma=False,
    )
```

```python
import functools

import jax
import jax.numpy as jnp
import ml_dtypes
import numpy as np
from jax import lax
from jax.experimental import pallas as pl
from jax.experimental.pallas import tpu as pltpu
from jax.sharding import PartitionSpec as P

HALF = 64
BLK = 2 * HALF
ROWS = 256
COLS = 2048
NB = COLS // BLK
EXT = COLS + BLK
CW = 256
MID = ROWS - BLK
EW = 512
DW = 512
NEAR = (0, 768, 1536, COLS)
PREP_MIB = 8
MID_MIB = 6
EDGE_MIB = 8
ZONAL_MIB = 16
UNROLL_B = 7
BF = jnp.bfloat16
F32 = jnp.float32


def taps_np():
    k = np.arange(-HALF, HALF + 1, dtype=np.float64)
    sigma = HALF / 2.0
    g = np.exp(-k * k / (2.0 * sigma * sigma))
    return g / g.sum()


def toeplitz(rows, cols, shift):
    g = taps_np()
    k = np.arange(cols)[None, :] - np.arange(rows)[:, None] + shift
    return np.where(np.abs(k) <= HALF, g[np.clip(k + HALF, 0, 2 * HALF)], 0.0)


def hi_lo(a):
    a = a.astype(np.float32)
    hi = a.astype(ml_dtypes.bfloat16)
    lo = (a - hi.astype(np.float32)).astype(ml_dtypes.bfloat16)
    return hi, lo


SCALE = float(1.0 / np.sum(taps_np() ** 2) ** 2)


def split(x):
    hi = x.astype(BF)
    lo = (x - hi.astype(F32)).astype(BF)
    return hi, lo


def dot(a, b):
    return jnp.dot(a, b, preferred_element_type=F32)


def five(u, v, t):
    return (u, v, t, u * t, v * t)


def fluxes(zh, zl, w, rows):
    r = dot(zh, w) + dot(zl, w)
    f = (r[:, :BLK] + r[:, BLK:]).reshape(5, rows, BLK)
    east = SCALE * (f[3] - f[0] * f[2])
    north = SCALE * (f[4] - f[1] * f[2])
    return pltpu.roll(east, HALF, 1), pltpu.roll(north, HALF, 1)


def merge(fo, start, left, right, rows):
    low = lax.broadcasted_iota(jnp.int32, (rows, BLK), 1) < HALF
    for q in range(2):
        fo[q, :, pl.ds(start, BLK)] = jnp.where(low, left[q], right[q])


def zonal_local(g, fields, store):
    for f, x in enumerate(fields):
        hi, lo = split(x)
        r = dot(g, hi)
        store(f, r[:ROWS] + r[ROWS:] + dot(g[:ROWS], lo))


def prep_kernel(core, u, v, t, m, x1, to_right, to_left, rows, wet_rows, cols, wet_cols, sem):
    top = pl.ds(pl.multiple_of(core[0] * (ROWS - HALF), HALF), HALF)
    sides = (pl.ds(COLS - BLK, BLK), pl.ds(0, BLK))
    copies = [pltpu.make_async_copy(m.at[top, :], wet_rows, sem.at[0, 3])]
    copies += [pltpu.make_async_copy(a.at[top, :], rows.at[i], sem.at[0, i]) for i, a in enumerate((u, v, t))]
    for s, side in enumerate(sides):
        copies.append(pltpu.make_async_copy(m.at[:, side], wet_cols.at[s], sem.at[1 + s, 3]))
        copies += [pltpu.make_async_copy(a.at[:, side], cols.at[s, i], sem.at[1 + s, i])
                   for i, a in enumerate((u, v, t))]
    for copy in copies:
        copy.start()
    for copy in copies[:4]:
        copy.wait()
    wet = wet_rows[...].astype(F32)
    for i in range(3):
        x1[i] = wet * rows[i]
    for s, out in enumerate((to_right, to_left)):
        for copy in copies[4 + 4 * s:8 + 4 * s]:
            copy.wait()
        wet = wet_cols[s].astype(F32)
        for i in range(3):
            out[i] = wet * cols[s, i]


def zonal_kernel(core, u, v, t, m, g_ref, zh, zl, zp, *refs):
    *near, ub, vb, tb, mb, sem = refs
    g = g_ref[...]
    lower = core[0] == 0

    def copies(j):
        cols = pl.ds(j * DW, DW)
        return [
            pltpu.make_async_copy(src.at[:, cols], dst.at[:, cols], sem.at[i, j])
            for i, (src, dst) in enumerate(((u, ub), (v, vb), (t, tb), (m, mb)))
        ]

    for j in range(2):
        for copy in copies(j):
            copy.start()
    for j in range(COLS // CW):
        if j * CW % DW == 0:
            k = j * CW // DW
            for copy in copies(k):
                copy.wait()
            if k + 2 < COLS // DW:
                for copy in copies(k + 2):
                    copy.start()
        cols = pl.ds(j * CW, CW)
        wet = mb[:, cols].astype(F32)
        three = (wet * ub[:, cols], wet * vb[:, cols], wet * tb[:, cols])
        part = max(p for p, start in enumerate(NEAR) if start <= j * CW)
        for i, x in enumerate(three):
            near[part][i, :, pl.ds(j * CW - NEAR[part], CW)] = jnp.where(lower, x[ROWS - HALF:], x[:HALF])

        def store(f, z):
            zp[f, 0:HALF, cols] = z[0:HALF]
            zp[f, HALF:BLK, cols] = z[ROWS - HALF:]
            a, b = split(z[HALF:ROWS - HALF])
            zh[f * MID:(f + 1) * MID, cols] = a
            zl[f * MID:(f + 1) * MID, cols] = b

        zonal_local(g, five(*three), store)


def flux_copies(fo, e_out, n_out, row, rows, start, width, sem):
    cols = pl.ds(start, width)
    return [
        pltpu.make_async_copy(fo.at[q, :, cols], out.at[pl.ds(row, rows), cols], sem.at[q])
        for q, out in enumerate((e_out, n_out))
    ]


def middle_kernel(zh, zl, from_left, from_right, g_ref, w_ref, e_out, n_out, zpw,
                  zwh, zwl, fo, carry, sem):
    w = w_ref[...]
    low = lax.broadcasted_iota(jnp.int32, (ROWS, BLK), 1) < HALF

    def store(f, z):
        zpw[f, 0:HALF] = z[0:HALF]
        zpw[f, HALF:BLK] = z[ROWS - HALF:]
        a, b = split(z[HALF:ROWS - HALF])
        zwh[f * MID:(f + 1) * MID] = a
        zwl[f * MID:(f + 1) * MID] = b

    zonal_local(g_ref[...], five(*[jnp.where(low, from_right[i], from_left[i]) for i in range(3)]), store)

    def two(j):
        cols = pl.ds(pl.multiple_of(j * BLK, BLK), 2 * BLK)
        return fluxes(zh[:, cols], zl[:, cols], w, MID)

    first = slice(0, BLK)
    last = slice(COLS - BLK, COLS)
    start = fluxes(jnp.concatenate([zwh[...], zh[:, first]], axis=1),
                   jnp.concatenate([zwl[...], zl[:, first]], axis=1), w, MID)
    for q in range(2):
        carry[q] = start[q]

    def step(j, _):
        a = two(2 * j)
        b = two(2 * j + 1)
        merge(fo, pl.multiple_of(j * CW, BLK), carry, a, MID)
        merge(fo, pl.multiple_of(j * CW + BLK, BLK), a, b, MID)
        for q in range(2):
            carry[q] = b[q]
        return 0

    lax.fori_loop(0, NB // 2 - 1, step, 0, unroll=UNROLL_B)
    early = flux_copies(fo, e_out, n_out, HALF, MID, 0, COLS - CW, sem.at[0])
    for copy in early:
        copy.start()
    a = two(NB - 2)
    merge(fo, COLS - CW, carry, a, MID)
    end = fluxes(jnp.concatenate([zh[:, last], zwh[...]], axis=1),
                 jnp.concatenate([zl[:, last], zwl[...]], axis=1), w, MID)
    merge(fo, COLS - BLK, a, end, MID)
    late = flux_copies(fo, e_out, n_out, HALF, MID, COLS - CW, CW, sem.at[1])
    for copy in late:
        copy.start()
    for copy in early + late:
        copy.wait()


def edge_kernel(npieces, *refs):
    sel_ref, e_in, n_in, zp, zpw = refs[:5]
    pieces = refs[5:5 + npieces]
    gx, w_ref, e_out, n_out, zh, zl, fo, carry, sem = refs[5 + npieces:]
    sel = sel_ref[0]
    w = w_ref[...]
    zrow = pl.ds(pl.multiple_of(sel * HALF, HALF), HALF)
    orow = pl.multiple_of(sel * (ROWS - HALF), HALF)
    gmat = gx[sel]

    def zonal(piece, cols, part, pcols, stores):
        for f, x in enumerate(five(piece[0, :, cols], piece[1, :, cols], piece[2, :, cols])):
            hi, lo = split(x)
            z = part[f, zrow, pcols] + dot(gmat, jnp.concatenate([hi, lo, hi], axis=0))
            a, b = split(z)
            for s in stores:
                zh[f * HALF:(f + 1) * HALF, s] = a
                zl[f * HALF:(f + 1) * HALF, s] = b

    def two(p):
        cols = pl.ds(p * BLK, 2 * BLK)
        return fluxes(zh[:, cols], zl[:, cols], w, HALF)

    n = pieces[-1].shape[2]
    zonal(pieces[-1], slice(n - BLK, n), zpw, slice(0, BLK), [slice(0, BLK), slice(COLS + BLK, COLS + CW)])
    base = 0
    for piece in pieces:
        n = min(piece.shape[2], COLS - base)
        for c in range(0, n, EW):
            k = min(EW, n - c)
            zonal(piece, slice(c, c + k), zp, slice(base + c, base + c + k), [slice(base + c + BLK, base + c + k + BLK)])
        base += n
    left = two(0)
    for b in range(NB):
        right = two(b + 1)
        merge(fo, b * BLK, left, right, HALF)
        left = right
        if b == NB - 3:
            early = flux_copies(fo, e_out, n_out, orow, HALF, 0, COLS - CW, sem.at[0])
            for copy in early:
                copy.start()
    late = flux_copies(fo, e_out, n_out, orow, HALF, COLS - CW, CW, sem.at[1])
    for copy in late:
        copy.start()
    for copy in early + late:
        copy.wait()


ANY = pl.BlockSpec(memory_space=pl.ANY)
HBM = pl.BlockSpec(memory_space=pltpu.HBM)
VMEM = pl.BlockSpec(memory_space=pltpu.VMEM)
SMEM = pl.BlockSpec(memory_space=pltpu.SMEM)
COST = pl.CostEstimate(flops=1_000_000, bytes_accessed=1_000_000, transcendentals=0)
FLUX = jax.ShapeDtypeStruct((ROWS, COLS), F32)


def params(mib):
    return pltpu.CompilerParams(vmem_limit_bytes=mib * 2**20)


def lat_matrix():
    hi, lo = hi_lo(toeplitz(BLK, 2 * BLK, -HALF).T)
    return jnp.asarray(np.concatenate([hi, lo], axis=1))


def lon_matrix():
    hi, lo = hi_lo(toeplitz(ROWS, ROWS, 0))
    return jnp.asarray(np.concatenate([hi, lo], axis=0))


def halo_matrix():
    mats = []
    for shift in (-HALF, HALF):
        hi, lo = hi_lo(toeplitz(HALF, HALF, shift))
        mats.append(np.concatenate([hi, hi, lo], axis=1))
    return jnp.asarray(np.stack(mats))


def prep(core, u, v, t, m):
    side = jax.ShapeDtypeStruct((3, ROWS, BLK), F32)
    return pl.pallas_call(
        prep_kernel,
        out_shape=(jax.ShapeDtypeStruct((3, HALF, COLS), F32), side, side),
        in_specs=[SMEM] + [HBM] * 4,
        out_specs=(VMEM,) * 3,
        scratch_shapes=[
            pltpu.VMEM((3, HALF, COLS), F32),
            pltpu.VMEM((HALF, COLS), jnp.int32),
            pltpu.VMEM((2, 3, ROWS, BLK), F32),
            pltpu.VMEM((2, ROWS, BLK), jnp.int32),
            pltpu.SemaphoreType.DMA((3, 4)),
        ],
        compiler_params=params(PREP_MIB),
        cost_estimate=COST,
        name="prep",
    )(core, u, v, t, m)


def zonal(core, u, v, t, m):
    half = jax.ShapeDtypeStruct((5 * MID, COLS), BF)
    near = [jax.ShapeDtypeStruct((3, HALF, b - a), F32) for a, b in zip(NEAR[:-1], NEAR[1:])]
    return pl.pallas_call(
        zonal_kernel,
        out_shape=(half, half, jax.ShapeDtypeStruct((5, BLK, COLS), F32), *near),
        in_specs=[SMEM] + [HBM] * 4 + [VMEM],
        out_specs=(VMEM,) * (3 + len(near)),
        scratch_shapes=[
            pltpu.VMEM((ROWS, COLS), F32),
            pltpu.VMEM((ROWS, COLS), F32),
            pltpu.VMEM((ROWS, COLS), F32),
            pltpu.VMEM((ROWS, COLS), jnp.int32),
            pltpu.SemaphoreType.DMA((4, COLS // DW)),
        ],
        compiler_params=params(ZONAL_MIB),
        cost_estimate=COST,
        name="zonal",
    )(core, u, v, t, m, lon_matrix())


def middle(zh, zl, from_left, from_right):
    return pl.pallas_call(
        middle_kernel,
        out_shape=(FLUX, FLUX, jax.ShapeDtypeStruct((5, BLK, BLK), F32)),
        in_specs=[VMEM] * 6,
        out_specs=(ANY, ANY, VMEM),
        scratch_shapes=[
            pltpu.VMEM((5 * MID, BLK), BF),
            pltpu.VMEM((5 * MID, BLK), BF),
            pltpu.VMEM((2, MID, COLS), F32),
            pltpu.VMEM((2, MID, BLK), F32),
            pltpu.SemaphoreType.DMA((2, 2)),
        ],
        compiler_params=params(MID_MIB),
        cost_estimate=COST,
        name="middle",
    )(zh, zl, from_left, from_right, lon_matrix(), lat_matrix())


def edge(sel, east, north, zp, zpw, pieces, name):
    return pl.pallas_call(
        functools.partial(edge_kernel, len(pieces)),
        out_shape=(FLUX, FLUX),
        in_specs=[SMEM, ANY, ANY] + [VMEM] * (4 + len(pieces)),
        out_specs=(ANY, ANY),
        scratch_shapes=[
            pltpu.VMEM((5 * HALF, COLS + CW), BF),
            pltpu.VMEM((5 * HALF, COLS + CW), BF),
            pltpu.VMEM((2, HALF, COLS), F32),
            pltpu.VMEM((2, HALF, BLK), F32),
            pltpu.SemaphoreType.DMA((2, 2)),
        ],
        input_output_aliases={1: 0, 2: 1},
        compiler_params=params(EDGE_MIB),
        cost_estimate=COST,
        name=name,
    )(sel, east, north, zp, zpw, *pieces, halo_matrix(), lat_matrix())


def shards(u, v, t, m):
    nlon, nlat = lax.axis_size("lon"), lax.axis_size("lat")
    core = lax.axis_index("lon") % 2
    xoff = core * (ROWS - HALF)
    ioff = (1 - core) * (ROWS - HALF)
    across = [(i, (i + 1) % nlon if i % 2 else (i - 1) % nlon) for i in range(nlon)]
    inside = [(i, i + 1 - 2 * (i % 2)) for i in range(nlon)]
    up = [(i, i + 1) for i in range(nlat - 1)]
    down = [(j, i) for i, j in up]

    sel = core.astype(jnp.int32).reshape(1)
    u, v, t, m = (pltpu.with_memory_space_constraint(a, pltpu.HBM) for a in (u, v, t, m))
    x1, to_right, to_left = prep(sel, u, v, t, m)
    x1 = lax.ppermute(x1, "lon", across)
    from_left = lax.ppermute(to_right, "lat", up)
    from_right = lax.ppermute(to_left, "lat", down)
    zh, zl, zp, *near = zonal(sel, u, v, t, m)
    zh, zl, from_left, from_right = lax.optimization_barrier((zh, zl, from_left, from_right))
    lane = lax.broadcasted_iota(jnp.int32, (3, HALF, BLK), 2)

    def corner(row):
        def cut(a):
            return lax.dynamic_slice(a, (0, row, 0), (3, HALF, BLK))

        return jnp.where(lane < HALF, cut(from_right), cut(from_left))

    x2 = corner(xoff)
    near[-1] = jnp.concatenate([near[-1], corner(ioff)], axis=2)
    x2, near, zh, zl = lax.optimization_barrier((x2, near, zh, zl))
    x2 = lax.ppermute(x2, "lon", across)
    near = [lax.ppermute(part, "lon", inside) for part in near]
    east, north, zpw = middle(zh, zl, from_left, from_right)
    east, north = edge(1 - sel, east, north, zp, zpw, near, "edge_near")
    return edge(sel, east, north, zp, zpw, (x1, x2), "edge_far")


def solution(mesh):
    return jax.shard_map(
        shards,
        mesh=mesh,
        in_specs=(P("lon", "lat"),) * 4,
        out_specs=(P("lon", "lat"),) * 2,
        check_vma=False,
    )
```

```python
import functools

import jax
import jax.numpy as jnp
import ml_dtypes
import numpy as np
from jax import lax
from jax.experimental import pallas as pl
from jax.experimental.pallas import tpu as pltpu
from jax.sharding import PartitionSpec as P

HALF = 64
BLK = 2 * HALF
ROWS = 256
COLS = 2048
NB = COLS // BLK
EXT = COLS + BLK
CW = 256
MID = ROWS - BLK
EW = 512
DW = 512
AHEAD = 2
NEAR = (0, 768, 1536, COLS)
PREP_MIB = 8
MID_MIB = 6
EDGE_MIB = 8
ZONAL_MIB = 16
UNROLL_B = 7
BF = jnp.bfloat16
F32 = jnp.float32


def taps_np():
    k = np.arange(-HALF, HALF + 1, dtype=np.float64)
    sigma = HALF / 2.0
    g = np.exp(-k * k / (2.0 * sigma * sigma))
    return g / g.sum()


def toeplitz(rows, cols, shift):
    g = taps_np()
    k = np.arange(cols)[None, :] - np.arange(rows)[:, None] + shift
    return np.where(np.abs(k) <= HALF, g[np.clip(k + HALF, 0, 2 * HALF)], 0.0)


def hi_lo(a):
    a = a.astype(np.float32)
    hi = a.astype(ml_dtypes.bfloat16)
    lo = (a - hi.astype(np.float32)).astype(ml_dtypes.bfloat16)
    return hi, lo


SCALE = float(1.0 / np.sum(taps_np() ** 2) ** 2)


def split(x):
    hi = x.astype(BF)
    lo = (x - hi.astype(F32)).astype(BF)
    return hi, lo


def dot(a, b):
    return jnp.dot(a, b, preferred_element_type=F32)


def five(u, v, t):
    return (u, v, t, u * t, v * t)


def fluxes(zh, zl, w, rows):
    r = dot(zh, w) + dot(zl, w)
    f = (r[:, :BLK] + r[:, BLK:]).reshape(5, rows, BLK)
    east = SCALE * (f[3] - f[0] * f[2])
    north = SCALE * (f[4] - f[1] * f[2])
    return pltpu.roll(east, HALF, 1), pltpu.roll(north, HALF, 1)


def merge(fo, start, left, right, rows):
    low = lax.broadcasted_iota(jnp.int32, (rows, BLK), 1) < HALF
    for q in range(2):
        fo[q, :, pl.ds(start, BLK)] = jnp.where(low, left[q], right[q])


def zonal_local(g, fields, store):
    for f, x in enumerate(fields):
        hi, lo = split(x)
        r = dot(g, hi)
        store(f, r[:ROWS] + r[ROWS:] + dot(g[:ROWS], lo))


def prep_kernel(where, u, v, t, m, x1, first, second, rows, wet_rows, cols, wet_cols, sem):
    top = pl.ds(pl.multiple_of(where[0] * (ROWS - HALF), HALF), HALF)
    odd = where[1]
    copies = [pltpu.make_async_copy(m.at[top, :], wet_rows, sem.at[0, 3])]
    copies += [pltpu.make_async_copy(a.at[top, :], rows.at[i], sem.at[0, i]) for i, a in enumerate((u, v, t))]
    for s, near_end in enumerate((odd, 1 - odd)):
        side = pl.ds(pl.multiple_of((1 - near_end) * (COLS - BLK), BLK), BLK)
        copies.append(pltpu.make_async_copy(m.at[:, side], wet_cols.at[s], sem.at[1 + s, 3]))
        copies += [pltpu.make_async_copy(a.at[:, side], cols.at[s, i], sem.at[1 + s, i])
                   for i, a in enumerate((u, v, t))]
    for copy in copies:
        copy.start()
    for copy in copies[:4]:
        copy.wait()
    wet = wet_rows[...].astype(F32)
    for i in range(3):
        x1[i] = wet * rows[i]
    low = lax.broadcasted_iota(jnp.int32, (BLK, BLK), 1) < HALF
    for s, (out, near_end) in enumerate(((first, odd), (second, 1 - odd))):
        for copy in copies[4 + 4 * s:8 + 4 * s]:
            copy.wait()
        wet = wet_cols[s].astype(F32)
        for i in range(3):
            x = wet * cols[s, i]
            y = pltpu.roll(x, HALF, 1)
            out[i] = jnp.where(
                near_end == 1,
                jnp.where(low, x[:BLK], y[BLK:]),
                jnp.where(low, y[:BLK], x[BLK:]),
            )


def corner_kernel(where, first, second, main, wrap, far, near):
    lower = where[0] == 0
    even = where[1] == 0
    low = lax.broadcasted_iota(jnp.int32, (BLK, BLK), 1) < HALF
    width = main.shape[2]
    near[:, :, 0:width] = main[...]
    for i in range(3):
        a, b = first[i], second[i]
        right = jnp.where(even, a, b)
        left = jnp.where(even, b, a)
        top = jnp.where(low, right, pltpu.roll(left, HALF, 1))
        bottom = jnp.where(low, pltpu.roll(right, HALF, 1), left)
        wrap[i, 0:BLK] = top
        wrap[i, BLK:ROWS] = bottom
        far[i] = jnp.where(lower, top[:HALF], bottom[HALF:])
        near[i, :, width:width + BLK] = jnp.where(lower, bottom[HALF:], top[:HALF])


def zonal_kernel(core, u, v, t, m, g_ref, zh, zl, zp, *refs):
    *near, ub, vb, tb, mb, sem = refs
    g = g_ref[...]
    lower = core[0] == 0

    def copies(j):
        cols = pl.ds(j * DW, DW)
        return [
            pltpu.make_async_copy(src.at[:, cols], dst.at[:, cols], sem.at[i, j])
            for i, (src, dst) in enumerate(((u, ub), (v, vb), (t, tb), (m, mb)))
        ]

    for j in range(AHEAD):
        for copy in copies(j):
            copy.start()
    for j in range(COLS // CW):
        if j * CW % DW == 0:
            k = j * CW // DW
            for copy in copies(k):
                copy.wait()
            if k + AHEAD < COLS // DW:
                for copy in copies(k + AHEAD):
                    copy.start()
        cols = pl.ds(j * CW, CW)
        wet = mb[:, cols].astype(F32)
        three = (wet * ub[:, cols], wet * vb[:, cols], wet * tb[:, cols])
        part = max(p for p, start in enumerate(NEAR) if start <= j * CW)
        for i, x in enumerate(three):
            near[part][i, :, pl.ds(j * CW - NEAR[part], CW)] = jnp.where(lower, x[ROWS - HALF:], x[:HALF])

        def store(f, z):
            zp[f, 0:HALF, cols] = z[0:HALF]
            zp[f, HALF:BLK, cols] = z[ROWS - HALF:]
            a, b = split(z[HALF:ROWS - HALF])
            zh[f * MID:(f + 1) * MID, cols] = a
            zl[f * MID:(f + 1) * MID, cols] = b

        zonal_local(g, five(*three), store)


def flux_copies(fo, e_out, n_out, row, rows, start, width, sem):
    cols = pl.ds(start, width)
    return [
        pltpu.make_async_copy(fo.at[q, :, cols], out.at[pl.ds(row, rows), cols], sem.at[q])
        for q, out in enumerate((e_out, n_out))
    ]


def middle_kernel(zh, zl, wrap, g_ref, w_ref, e_out, n_out, zpw,
                  zwh, zwl, fo, carry, sem):
    w = w_ref[...]

    def store(f, z):
        zpw[f, 0:HALF] = z[0:HALF]
        zpw[f, HALF:BLK] = z[ROWS - HALF:]
        a, b = split(z[HALF:ROWS - HALF])
        zwh[f * MID:(f + 1) * MID] = a
        zwl[f * MID:(f + 1) * MID] = b

    zonal_local(g_ref[...], five(wrap[0], wrap[1], wrap[2]), store)

    def two(j):
        cols = pl.ds(pl.multiple_of(j * BLK, BLK), 2 * BLK)
        return fluxes(zh[:, cols], zl[:, cols], w, MID)

    first = slice(0, BLK)
    last = slice(COLS - BLK, COLS)
    start = fluxes(jnp.concatenate([zwh[...], zh[:, first]], axis=1),
                   jnp.concatenate([zwl[...], zl[:, first]], axis=1), w, MID)
    for q in range(2):
        carry[q] = start[q]

    def step(j, _):
        a = two(2 * j)
        b = two(2 * j + 1)
        merge(fo, pl.multiple_of(j * CW, BLK), carry, a, MID)
        merge(fo, pl.multiple_of(j * CW + BLK, BLK), a, b, MID)
        for q in range(2):
            carry[q] = b[q]
        return 0

    lax.fori_loop(0, NB // 2 - 1, step, 0, unroll=UNROLL_B)
    early = flux_copies(fo, e_out, n_out, HALF, MID, 0, COLS - CW, sem.at[0])
    for copy in early:
        copy.start()
    a = two(NB - 2)
    merge(fo, COLS - CW, carry, a, MID)
    end = fluxes(jnp.concatenate([zh[:, last], zwh[...]], axis=1),
                 jnp.concatenate([zl[:, last], zwl[...]], axis=1), w, MID)
    merge(fo, COLS - BLK, a, end, MID)
    late = flux_copies(fo, e_out, n_out, HALF, MID, COLS - CW, CW, sem.at[1])
    for copy in late:
        copy.start()
    for copy in early + late:
        copy.wait()


def edge_kernel(npieces, *refs):
    sel_ref, e_in, n_in, zp, zpw = refs[:5]
    pieces = refs[5:5 + npieces]
    gx, w_ref, e_out, n_out, zh, zl, fo, carry, sem = refs[5 + npieces:]
    sel = sel_ref[0]
    w = w_ref[...]
    zrow = pl.ds(pl.multiple_of(sel * HALF, HALF), HALF)
    orow = pl.multiple_of(sel * (ROWS - HALF), HALF)
    gmat = gx[sel]

    def zonal(piece, cols, part, pcols, stores):
        for f, x in enumerate(five(piece[0, :, cols], piece[1, :, cols], piece[2, :, cols])):
            hi, lo = split(x)
            z = part[f, zrow, pcols] + dot(gmat, jnp.concatenate([hi, lo, hi], axis=0))
            a, b = split(z)
            for s in stores:
                zh[f * HALF:(f + 1) * HALF, s] = a
                zl[f * HALF:(f + 1) * HALF, s] = b

    def two(p):
        cols = pl.ds(p * BLK, 2 * BLK)
        return fluxes(zh[:, cols], zl[:, cols], w, HALF)

    n = pieces[-1].shape[2]
    zonal(pieces[-1], slice(n - BLK, n), zpw, slice(0, BLK), [slice(0, BLK), slice(COLS + BLK, COLS + CW)])
    base = 0
    for piece in pieces:
        n = min(piece.shape[2], COLS - base)
        for c in range(0, n, EW):
            k = min(EW, n - c)
            zonal(piece, slice(c, c + k), zp, slice(base + c, base + c + k), [slice(base + c + BLK, base + c + k + BLK)])
        base += n
    left = two(0)
    for b in range(NB):
        right = two(b + 1)
        merge(fo, b * BLK, left, right, HALF)
        left = right
        if b == NB - 3:
            early = flux_copies(fo, e_out, n_out, orow, HALF, 0, COLS - CW, sem.at[0])
            for copy in early:
                copy.start()
    late = flux_copies(fo, e_out, n_out, orow, HALF, COLS - CW, CW, sem.at[1])
    for copy in late:
        copy.start()
    for copy in early + late:
        copy.wait()


ANY = pl.BlockSpec(memory_space=pl.ANY)
HBM = pl.BlockSpec(memory_space=pltpu.HBM)
VMEM = pl.BlockSpec(memory_space=pltpu.VMEM)
SMEM = pl.BlockSpec(memory_space=pltpu.SMEM)
COST = pl.CostEstimate(flops=1_000_000, bytes_accessed=1_000_000, transcendentals=0)
FLUX = jax.ShapeDtypeStruct((ROWS, COLS), F32)


def params(mib):
    return pltpu.CompilerParams(vmem_limit_bytes=mib * 2**20)


def lat_matrix():
    hi, lo = hi_lo(toeplitz(BLK, 2 * BLK, -HALF).T)
    return jnp.asarray(np.concatenate([hi, lo], axis=1))


def lon_matrix():
    hi, lo = hi_lo(toeplitz(ROWS, ROWS, 0))
    return jnp.asarray(np.concatenate([hi, lo], axis=0))


def halo_matrix():
    mats = []
    for shift in (-HALF, HALF):
        hi, lo = hi_lo(toeplitz(HALF, HALF, shift))
        mats.append(np.concatenate([hi, hi, lo], axis=1))
    return jnp.asarray(np.stack(mats))


def prep(core, u, v, t, m):
    side = jax.ShapeDtypeStruct((3, BLK, BLK), F32)
    return pl.pallas_call(
        prep_kernel,
        out_shape=(jax.ShapeDtypeStruct((3, HALF, COLS), F32), side, side),
        in_specs=[SMEM] + [HBM] * 4,
        out_specs=(VMEM,) * 3,
        scratch_shapes=[
            pltpu.VMEM((3, HALF, COLS), F32),
            pltpu.VMEM((HALF, COLS), jnp.int32),
            pltpu.VMEM((2, 3, ROWS, BLK), F32),
            pltpu.VMEM((2, ROWS, BLK), jnp.int32),
            pltpu.SemaphoreType.DMA((3, 4)),
        ],
        compiler_params=params(PREP_MIB),
        cost_estimate=COST,
        name="prep",
    )(core, u, v, t, m)


def corners(where, first, second, main):
    return pl.pallas_call(
        corner_kernel,
        out_shape=(
            jax.ShapeDtypeStruct((3, ROWS, BLK), F32),
            jax.ShapeDtypeStruct((3, HALF, BLK), F32),
            jax.ShapeDtypeStruct((3, HALF, main.shape[2] + BLK), F32),
        ),
        in_specs=[SMEM] + [VMEM] * 3,
        out_specs=(VMEM,) * 3,
        compiler_params=params(2),
        cost_estimate=COST,
        name="corners",
    )(where, first, second, main)


def zonal(core, u, v, t, m):
    half = jax.ShapeDtypeStruct((5 * MID, COLS), BF)
    near = [jax.ShapeDtypeStruct((3, HALF, b - a), F32) for a, b in zip(NEAR[:-1], NEAR[1:])]
    return pl.pallas_call(
        zonal_kernel,
        out_shape=(half, half, jax.ShapeDtypeStruct((5, BLK, COLS), F32), *near),
        in_specs=[SMEM] + [HBM] * 4 + [VMEM],
        out_specs=(VMEM,) * (3 + len(near)),
        scratch_shapes=[
            pltpu.VMEM((ROWS, COLS), F32),
            pltpu.VMEM((ROWS, COLS), F32),
            pltpu.VMEM((ROWS, COLS), F32),
            pltpu.VMEM((ROWS, COLS), jnp.int32),
            pltpu.SemaphoreType.DMA((4, COLS // DW)),
        ],
        compiler_params=params(ZONAL_MIB),
        cost_estimate=COST,
        name="zonal",
    )(core, u, v, t, m, lon_matrix())


def middle(zh, zl, wrap):
    return pl.pallas_call(
        middle_kernel,
        out_shape=(FLUX, FLUX, jax.ShapeDtypeStruct((5, BLK, BLK), F32)),
        in_specs=[VMEM] * 5,
        out_specs=(ANY, ANY, VMEM),
        scratch_shapes=[
            pltpu.VMEM((5 * MID, BLK), BF),
            pltpu.VMEM((5 * MID, BLK), BF),
            pltpu.VMEM((2, MID, COLS), F32),
            pltpu.VMEM((2, MID, BLK), F32),
            pltpu.SemaphoreType.DMA((2, 2)),
        ],
        compiler_params=params(MID_MIB),
        cost_estimate=COST,
        name="middle",
    )(zh, zl, wrap, lon_matrix(), lat_matrix())


def edge(sel, east, north, zp, zpw, pieces, name):
    return pl.pallas_call(
        functools.partial(edge_kernel, len(pieces)),
        out_shape=(FLUX, FLUX),
        in_specs=[SMEM, ANY, ANY] + [VMEM] * (4 + len(pieces)),
        out_specs=(ANY, ANY),
        scratch_shapes=[
            pltpu.VMEM((5 * HALF, COLS + CW), BF),
            pltpu.VMEM((5 * HALF, COLS + CW), BF),
            pltpu.VMEM((2, HALF, COLS), F32),
            pltpu.VMEM((2, HALF, BLK), F32),
            pltpu.SemaphoreType.DMA((2, 2)),
        ],
        input_output_aliases={1: 0, 2: 1},
        compiler_params=params(EDGE_MIB),
        cost_estimate=COST,
        name=name,
    )(sel, east, north, zp, zpw, *pieces, halo_matrix(), lat_matrix())


def shards(u, v, t, m):
    nlon, nlat = lax.axis_size("lon"), lax.axis_size("lat")
    core = lax.axis_index("lon") % 2
    across = [(i, (i + 1) % nlon if i % 2 else (i - 1) % nlon) for i in range(nlon)]
    inside = [(i, i + 1 - 2 * (i % 2)) for i in range(nlon)]
    odd = lax.axis_index("lat") % 2
    even_pairs = [(i, i + 1 - 2 * (i % 2)) for i in range(nlat)]
    odd_pairs = [(i, i - 1 + 2 * (i % 2)) for i in range(1, nlat - 1)]

    sel = core.astype(jnp.int32).reshape(1)
    u, v, t, m = (pltpu.with_memory_space_constraint(a, pltpu.HBM) for a in (u, v, t, m))
    where = jnp.stack([core, odd]).astype(jnp.int32)
    x1, first, second = prep(where, u, v, t, m)
    x1 = lax.ppermute(x1, "lon", across)
    first = lax.ppermute(first, "lat", even_pairs)
    second = lax.ppermute(second, "lat", odd_pairs)
    zh, zl, zp, *near = zonal(sel, u, v, t, m)
    zh, zl, first, second = lax.optimization_barrier((zh, zl, first, second))
    wrap, x2, near[-1] = corners(where, first, second, near[-1])
    x2, near, zh, zl = lax.optimization_barrier((x2, near, zh, zl))
    x2 = lax.ppermute(x2, "lon", across)
    near = [lax.ppermute(part, "lon", inside) for part in near]
    east, north, zpw = middle(zh, zl, wrap)
    east, north = edge(1 - sel, east, north, zp, zpw, near, "edge_near")
    return edge(sel, east, north, zp, zpw, (x1, x2), "edge_far")


def solution(mesh):
    return jax.shard_map(
        shards,
        mesh=mesh,
        in_specs=(P("lon", "lat"),) * 4,
        out_specs=(P("lon", "lat"),) * 2,
        check_vma=False,
    )
```

```python
import functools

import jax
import jax.numpy as jnp
import ml_dtypes
import numpy as np
from jax import lax
from jax.experimental import pallas as pl
from jax.experimental.pallas import tpu as pltpu
from jax.sharding import PartitionSpec as P

HALF = 64
BLK = 2 * HALF
ROWS = 256
COLS = 2048
NB = COLS // BLK
EXT = COLS + BLK
CW = 256
MID = ROWS - BLK
EW = 512
NEAR = (0, 768, 1536, COLS)
PREP_MIB = 8
MID_MIB = 6
EDGE_MIB = 8
ZONAL_MIB = 6
UNROLL_B = 7
BF = jnp.bfloat16
F32 = jnp.float32


def taps_np():
    k = np.arange(-HALF, HALF + 1, dtype=np.float64)
    sigma = HALF / 2.0
    g = np.exp(-k * k / (2.0 * sigma * sigma))
    return g / g.sum()


def toeplitz(rows, cols, shift):
    g = taps_np()
    k = np.arange(cols)[None, :] - np.arange(rows)[:, None] + shift
    return np.where(np.abs(k) <= HALF, g[np.clip(k + HALF, 0, 2 * HALF)], 0.0)


def hi_lo(a):
    a = a.astype(np.float32)
    hi = a.astype(ml_dtypes.bfloat16)
    lo = (a - hi.astype(np.float32)).astype(ml_dtypes.bfloat16)
    return hi, lo


SCALE = float(1.0 / np.sum(taps_np() ** 2) ** 2)


def split(x):
    hi = x.astype(BF)
    lo = (x - hi.astype(F32)).astype(BF)
    return hi, lo


def dot(a, b):
    return jnp.dot(a, b, preferred_element_type=F32)


def five(u, v, t):
    return (u, v, t, u * t, v * t)


def fluxes(zh, zl, w, rows):
    r = dot(zh, w) + dot(zl, w)
    f = (r[:, :BLK] + r[:, BLK:]).reshape(5, rows, BLK)
    east = SCALE * (f[3] - f[0] * f[2])
    north = SCALE * (f[4] - f[1] * f[2])
    return pltpu.roll(east, HALF, 1), pltpu.roll(north, HALF, 1)


def merge(fo, start, left, right, rows):
    low = lax.broadcasted_iota(jnp.int32, (rows, BLK), 1) < HALF
    for q in range(2):
        fo[q, :, pl.ds(start, BLK)] = jnp.where(low, left[q], right[q])


def zonal_local(g, fields, store):
    for f, x in enumerate(fields):
        hi, lo = split(x)
        r = dot(g, hi)
        store(f, r[:ROWS] + r[ROWS:] + dot(g[:ROWS], lo))


def prep_kernel(where, u, v, t, m, g, x1, first, second, g_out, rows, wet_rows, cols, wet_cols, sem):
    top = pl.ds(pl.multiple_of(where[0] * (ROWS - HALF), HALF), HALF)
    odd = where[1]
    copies = [pltpu.make_async_copy(m.at[top, :], wet_rows, sem.at[0, 3])]
    copies += [pltpu.make_async_copy(a.at[top, :], rows.at[i], sem.at[0, i]) for i, a in enumerate((u, v, t))]
    for s, near_end in enumerate((odd, 1 - odd)):
        side = pl.ds(pl.multiple_of((1 - near_end) * (COLS - BLK), BLK), BLK)
        copies.append(pltpu.make_async_copy(m.at[:, side], wet_cols.at[s], sem.at[1 + s, 3]))
        copies += [pltpu.make_async_copy(a.at[:, side], cols.at[s, i], sem.at[1 + s, i])
                   for i, a in enumerate((u, v, t))]
    for copy in copies:
        copy.start()
    g_copy = pltpu.make_async_copy(g, g_out, sem.at[3, 0])
    g_copy.start()
    for copy in copies[:4]:
        copy.wait()
    wet = wet_rows[...].astype(F32)
    for i in range(3):
        x1[i] = wet * rows[i]
    low = lax.broadcasted_iota(jnp.int32, (BLK, BLK), 1) < HALF
    for s, (out, near_end) in enumerate(((first, odd), (second, 1 - odd))):
        for copy in copies[4 + 4 * s:8 + 4 * s]:
            copy.wait()
        wet = wet_cols[s].astype(F32)
        for i in range(3):
            x = wet * cols[s, i]
            y = pltpu.roll(x, HALF, 1)
            out[i] = jnp.where(
                near_end == 1,
                jnp.where(low, x[:BLK], y[BLK:]),
                jnp.where(low, y[:BLK], x[BLK:]),
            )
    g_copy.wait()


def corner_kernel(where, first, second, main, wrap, far, near):
    lower = where[0] == 0
    even = where[1] == 0
    low = lax.broadcasted_iota(jnp.int32, (BLK, BLK), 1) < HALF
    width = main.shape[2]
    near[:, :, 0:width] = main[...]
    for i in range(3):
        a, b = first[i], second[i]
        right = jnp.where(even, a, b)
        left = jnp.where(even, b, a)
        top = jnp.where(low, right, pltpu.roll(left, HALF, 1))
        bottom = jnp.where(low, pltpu.roll(right, HALF, 1), left)
        wrap[i, 0:BLK] = top
        wrap[i, BLK:ROWS] = bottom
        far[i] = jnp.where(lower, top[:HALF], bottom[HALF:])
        near[i, :, width:width + BLK] = jnp.where(lower, bottom[HALF:], top[:HALF])


def zonal_kernel(core, u, v, t, m, g_ref, zh, zl, zp, *refs):
    near = refs
    g = g_ref[...]
    lower = core[0] == 0

    for j in range(COLS // CW):
        cols = pl.ds(j * CW, CW)
        wet = m[:, cols].astype(F32)
        three = (wet * u[:, cols], wet * v[:, cols], wet * t[:, cols])
        part = max(p for p, start in enumerate(NEAR) if start <= j * CW)
        for i, x in enumerate(three):
            near[part][i, :, pl.ds(j * CW - NEAR[part], CW)] = jnp.where(lower, x[ROWS - HALF:], x[:HALF])

        def store(f, z):
            zp[f, 0:HALF, cols] = z[0:HALF]
            zp[f, HALF:BLK, cols] = z[ROWS - HALF:]
            a, b = split(z[HALF:ROWS - HALF])
            zh[f * MID:(f + 1) * MID, cols] = a
            zl[f * MID:(f + 1) * MID, cols] = b

        zonal_local(g, five(*three), store)


def flux_copies(fo, e_out, n_out, row, rows, start, width, sem):
    cols = pl.ds(start, width)
    return [
        pltpu.make_async_copy(fo.at[q, :, cols], out.at[pl.ds(row, rows), cols], sem.at[q])
        for q, out in enumerate((e_out, n_out))
    ]


def middle_kernel(zh, zl, wrap, g_ref, w_ref, e_out, n_out, zpw,
                  zwh, zwl, fo, carry, sem):
    w = w_ref[...]

    def store(f, z):
        zpw[f, 0:HALF] = z[0:HALF]
        zpw[f, HALF:BLK] = z[ROWS - HALF:]
        a, b = split(z[HALF:ROWS - HALF])
        zwh[f * MID:(f + 1) * MID] = a
        zwl[f * MID:(f + 1) * MID] = b

    zonal_local(g_ref[...], five(wrap[0], wrap[1], wrap[2]), store)

    def two(j):
        cols = pl.ds(pl.multiple_of(j * BLK, BLK), 2 * BLK)
        return fluxes(zh[:, cols], zl[:, cols], w, MID)

    first = slice(0, BLK)
    last = slice(COLS - BLK, COLS)
    start = fluxes(jnp.concatenate([zwh[...], zh[:, first]], axis=1),
                   jnp.concatenate([zwl[...], zl[:, first]], axis=1), w, MID)
    for q in range(2):
        carry[q] = start[q]

    def step(j, _):
        a = two(2 * j)
        b = two(2 * j + 1)
        merge(fo, pl.multiple_of(j * CW, BLK), carry, a, MID)
        merge(fo, pl.multiple_of(j * CW + BLK, BLK), a, b, MID)
        for q in range(2):
            carry[q] = b[q]
        return 0

    lax.fori_loop(0, NB // 2 - 1, step, 0, unroll=UNROLL_B)
    early = flux_copies(fo, e_out, n_out, HALF, MID, 0, COLS - CW, sem.at[0])
    for copy in early:
        copy.start()
    a = two(NB - 2)
    merge(fo, COLS - CW, carry, a, MID)
    end = fluxes(jnp.concatenate([zh[:, last], zwh[...]], axis=1),
                 jnp.concatenate([zl[:, last], zwl[...]], axis=1), w, MID)
    merge(fo, COLS - BLK, a, end, MID)
    late = flux_copies(fo, e_out, n_out, HALF, MID, COLS - CW, CW, sem.at[1])
    for copy in late:
        copy.start()
    for copy in early + late:
        copy.wait()


def edge_kernel(npieces, *refs):
    sel_ref, e_in, n_in, zp, zpw = refs[:5]
    pieces = refs[5:5 + npieces]
    gx, w_ref, e_out, n_out, zh, zl, fo, carry, sem = refs[5 + npieces:]
    sel = sel_ref[0]
    w = w_ref[...]
    zrow = pl.ds(pl.multiple_of(sel * HALF, HALF), HALF)
    orow = pl.multiple_of(sel * (ROWS - HALF), HALF)
    gmat = gx[sel]

    def zonal(piece, cols, part, pcols, stores):
        for f, x in enumerate(five(piece[0, :, cols], piece[1, :, cols], piece[2, :, cols])):
            hi, lo = split(x)
            z = part[f, zrow, pcols] + dot(gmat, jnp.concatenate([hi, lo, hi], axis=0))
            a, b = split(z)
            for s in stores:
                zh[f * HALF:(f + 1) * HALF, s] = a
                zl[f * HALF:(f + 1) * HALF, s] = b

    def two(p):
        cols = pl.ds(p * BLK, 2 * BLK)
        return fluxes(zh[:, cols], zl[:, cols], w, HALF)

    n = pieces[-1].shape[2]
    zonal(pieces[-1], slice(n - BLK, n), zpw, slice(0, BLK), [slice(0, BLK), slice(COLS + BLK, COLS + CW)])
    base = 0
    for piece in pieces:
        n = min(piece.shape[2], COLS - base)
        for c in range(0, n, EW):
            k = min(EW, n - c)
            zonal(piece, slice(c, c + k), zp, slice(base + c, base + c + k), [slice(base + c + BLK, base + c + k + BLK)])
        base += n
    left = two(0)
    for b in range(NB):
        right = two(b + 1)
        merge(fo, b * BLK, left, right, HALF)
        left = right
        if b == NB - 3:
            early = flux_copies(fo, e_out, n_out, orow, HALF, 0, COLS - CW, sem.at[0])
            for copy in early:
                copy.start()
    late = flux_copies(fo, e_out, n_out, orow, HALF, COLS - CW, CW, sem.at[1])
    for copy in late:
        copy.start()
    for copy in early + late:
        copy.wait()


ANY = pl.BlockSpec(memory_space=pl.ANY)
HBM = pl.BlockSpec(memory_space=pltpu.HBM)
VMEM = pl.BlockSpec(memory_space=pltpu.VMEM)
SMEM = pl.BlockSpec(memory_space=pltpu.SMEM)
COST = pl.CostEstimate(flops=1_000_000, bytes_accessed=1_000_000, transcendentals=0)
FLUX = jax.ShapeDtypeStruct((ROWS, COLS), F32)


def params(mib):
    return pltpu.CompilerParams(vmem_limit_bytes=mib * 2**20)


def lat_matrix():
    hi, lo = hi_lo(toeplitz(BLK, 2 * BLK, -HALF).T)
    return jnp.asarray(np.concatenate([hi, lo], axis=1))


def lon_matrix():
    hi, lo = hi_lo(toeplitz(ROWS, ROWS, 0))
    return jnp.asarray(np.concatenate([hi, lo], axis=0))


def halo_matrix():
    mats = []
    for shift in (-HALF, HALF):
        hi, lo = hi_lo(toeplitz(HALF, HALF, shift))
        mats.append(np.concatenate([hi, hi, lo], axis=1))
    return jnp.asarray(np.stack(mats))


def prep(core, u, v, t, m, g):
    side = jax.ShapeDtypeStruct((3, BLK, BLK), F32)
    return pl.pallas_call(
        prep_kernel,
        out_shape=(jax.ShapeDtypeStruct((3, HALF, COLS), F32), side, side, jax.ShapeDtypeStruct(g.shape, BF)),
        in_specs=[SMEM] + [HBM] * 5,
        out_specs=(VMEM,) * 4,
        scratch_shapes=[
            pltpu.VMEM((3, HALF, COLS), F32),
            pltpu.VMEM((HALF, COLS), jnp.int32),
            pltpu.VMEM((2, 3, ROWS, BLK), F32),
            pltpu.VMEM((2, ROWS, BLK), jnp.int32),
            pltpu.SemaphoreType.DMA((4, 4)),
        ],
        compiler_params=params(PREP_MIB),
        cost_estimate=pl.CostEstimate(flops=1_000_000, bytes_accessed=60_000_000, transcendentals=0),
        name="prep",
    )(core, u, v, t, m, g)


def corners(where, first, second, main):
    return pl.pallas_call(
        corner_kernel,
        out_shape=(
            jax.ShapeDtypeStruct((3, ROWS, BLK), F32),
            jax.ShapeDtypeStruct((3, HALF, BLK), F32),
            jax.ShapeDtypeStruct((3, HALF, main.shape[2] + BLK), F32),
        ),
        in_specs=[SMEM] + [VMEM] * 3,
        out_specs=(VMEM,) * 3,
        compiler_params=params(2),
        cost_estimate=COST,
        name="corners",
    )(where, first, second, main)


def zonal(core, u, v, t, m, g):
    half = jax.ShapeDtypeStruct((5 * MID, COLS), BF)
    near = [jax.ShapeDtypeStruct((3, HALF, b - a), F32) for a, b in zip(NEAR[:-1], NEAR[1:])]
    return pl.pallas_call(
        zonal_kernel,
        out_shape=(half, half, jax.ShapeDtypeStruct((5, BLK, COLS), F32), *near),
        in_specs=[SMEM] + [VMEM] * 5,
        out_specs=(VMEM,) * (3 + len(near)),
        compiler_params=params(ZONAL_MIB),
        cost_estimate=COST,
        name="zonal",
    )(core, u, v, t, m, g)


def middle(zh, zl, wrap, g):
    return pl.pallas_call(
        middle_kernel,
        out_shape=(FLUX, FLUX, jax.ShapeDtypeStruct((5, BLK, BLK), F32)),
        in_specs=[VMEM] * 5,
        out_specs=(ANY, ANY, VMEM),
        scratch_shapes=[
            pltpu.VMEM((5 * MID, BLK), BF),
            pltpu.VMEM((5 * MID, BLK), BF),
            pltpu.VMEM((2, MID, COLS), F32),
            pltpu.VMEM((2, MID, BLK), F32),
            pltpu.SemaphoreType.DMA((2, 2)),
        ],
        compiler_params=params(MID_MIB),
        cost_estimate=COST,
        name="middle",
    )(zh, zl, wrap, g, lat_matrix())


def edge(sel, east, north, zp, zpw, pieces, name):
    return pl.pallas_call(
        functools.partial(edge_kernel, len(pieces)),
        out_shape=(FLUX, FLUX),
        in_specs=[SMEM, ANY, ANY] + [VMEM] * (4 + len(pieces)),
        out_specs=(ANY, ANY),
        scratch_shapes=[
            pltpu.VMEM((5 * HALF, COLS + CW), BF),
            pltpu.VMEM((5 * HALF, COLS + CW), BF),
            pltpu.VMEM((2, HALF, COLS), F32),
            pltpu.VMEM((2, HALF, BLK), F32),
            pltpu.SemaphoreType.DMA((2, 2)),
        ],
        input_output_aliases={1: 0, 2: 1},
        compiler_params=params(EDGE_MIB),
        cost_estimate=COST,
        name=name,
    )(sel, east, north, zp, zpw, *pieces, halo_matrix(), lat_matrix())


def shards(u, v, t, m):
    nlon, nlat = lax.axis_size("lon"), lax.axis_size("lat")
    core = lax.axis_index("lon") % 2
    across = [(i, (i + 1) % nlon if i % 2 else (i - 1) % nlon) for i in range(nlon)]
    inside = [(i, i + 1 - 2 * (i % 2)) for i in range(nlon)]
    odd = lax.axis_index("lat") % 2
    even_pairs = [(i, i + 1 - 2 * (i % 2)) for i in range(nlat)]
    odd_pairs = [(i, i - 1 + 2 * (i % 2)) for i in range(1, nlat - 1)]

    sel = core.astype(jnp.int32).reshape(1)
    held = [pltpu.with_memory_space_constraint(a, pltpu.HBM) for a in (u, v, t, m, lon_matrix())]
    where = jnp.stack([core, odd]).astype(jnp.int32)
    x1, first, second, g = prep(where, *held)
    x1 = lax.ppermute(x1, "lon", across)
    first = lax.ppermute(first, "lat", even_pairs)
    second = lax.ppermute(second, "lat", odd_pairs)
    zh, zl, zp, *near = zonal(sel, u, v, t, m, g)
    zh, zl, first, second = lax.optimization_barrier((zh, zl, first, second))
    wrap, x2, near[-1] = corners(where, first, second, near[-1])
    x2, near, zh, zl = lax.optimization_barrier((x2, near, zh, zl))
    x2 = lax.ppermute(x2, "lon", across)
    near = [lax.ppermute(part, "lon", inside) for part in near]
    east, north, zpw = middle(zh, zl, wrap, g)
    east, north = edge(1 - sel, east, north, zp, zpw, near, "edge_near")
    return edge(sel, east, north, zp, zpw, (x1, x2), "edge_far")


def solution(mesh):
    return jax.shard_map(
        shards,
        mesh=mesh,
        in_specs=(P("lon", "lat"),) * 4,
        out_specs=(P("lon", "lat"),) * 2,
        check_vma=False,
    )
```
